128 devices in a mesh: dp: 32 (over x, y, core), tensor: 4 (over z).
Axes of the slice: x: 4, y: 4, z: 4, core: 2. Of those that a mesh axis runs over, the one named last changes fastest.
Arguments:
- gradient: bfloat16 [8192, 16384], P('dp', 'tensor')
- block_slot: int32 [8, 4, 4], replicated, may hold values from 0 to 3, as said below
- left_factor: float32 [128, 1024, 1024], P(('dp', 'tensor')), as said below
- right_factor: float32 [128, 1024, 1024], P(('dp', 'tensor')), as said below
- left_root: bfloat16 [128, 1024, 1024], P(('dp', 'tensor')), as said below
- right_root: bfloat16 [128, 1024, 1024], P(('dp', 'tensor')), as said below
Outputs:
- update: bfloat16 [8192, 16384], P('dp', 'tensor')
- new_left: float32 [128, 1024, 1024], P(('dp', 'tensor'))
- new_right: float32 [128, 1024, 1024], P(('dp', 'tensor'))
The draws below stay inside these ranges and needn't reach their ends.
Inputs may be any that keep to these rules, and one draw needn't show every extreme that they name: For each row block and each tensor index e, block_slot[i, e, :] is a permutation of 0 to 3. `left_factor`: every block is symmetric. `right_factor`: every block is symmetric. `left_root`: every block is symmetric. `right_root`: every block is symmetric.
All inputs are finite; a program needn't handle non-finite values.
Results may differ from the reference program's by a relative error of at most 0.0049.
Values may be sent and summed in bfloat16 or wider, within the bound.
A program may use at most 128 MiB of HBM per device.

```python
import math
import jax
import jax.numpy as jnp
from jax import lax

D = 8192
B = 1024
COLS = 16384
BLOCKS = 128
N_DP = 32
N_TENSOR = 4


def symmetric_blocks(key, lowest, highest, spread):
    noise_key, diagonal_key = jax.random.split(key)
    noise = jax.random.normal(noise_key, (BLOCKS, B, B), jnp.float32) * spread
    diagonal = jnp.exp(jax.random.uniform(diagonal_key, (BLOCKS, B), jnp.float32, math.log(lowest), math.log(highest)))
    return noise + jnp.swapaxes(noise, 1, 2) + jnp.eye(B, dtype=jnp.float32)[None] * diagonal[:, :, None]


def draw_gradient(key, part):
    key = jax.random.fold_in(key, 11)
    base_key, row_key, col_key = jax.random.split(key, 3)
    row_scale = jnp.exp(jax.random.uniform(row_key, (D, 1), jnp.float32, 0.0, 1.2))
    col_scale = jnp.exp(jax.random.uniform(col_key, (1, COLS), jnp.float32, 0.0, 1.2))
    base = jax.random.normal(base_key, (D, COLS), jnp.float32)
    return (0.03 * base * row_scale * col_scale).astype(jnp.bfloat16)


def draw_block_slot(key, part):
    key = jax.random.fold_in(key, 12)
    keys = jax.random.split(key, D // B * N_TENSOR)
    perms = jax.vmap(lambda single: jax.random.permutation(single, N_TENSOR))(keys)
    return perms.reshape(D // B, N_TENSOR, N_TENSOR).astype(jnp.int32)


def draw_left_factor(key, part):
    key = jax.random.fold_in(key, 13)
    return symmetric_blocks(key, 5.0, 50.0, 1.4 / math.sqrt(B))


def draw_right_factor(key, part):
    key = jax.random.fold_in(key, 14)
    return symmetric_blocks(key, 5.0, 50.0, 1.4 / math.sqrt(B))


def draw_left_root(key, part):
    key = jax.random.fold_in(key, 15)
    return symmetric_blocks(key, 0.6, 1.8, 0.27 / math.sqrt(2.0 * B)).astype(jnp.bfloat16)


def draw_right_root(key, part):
    key = jax.random.fold_in(key, 16)
    return symmetric_blocks(key, 0.6, 1.8, 0.27 / math.sqrt(2.0 * B)).astype(jnp.bfloat16)


def setup_inputs(seed: int = 0) -> dict:
    splits = jax.random.split(jax.random.key(seed), 7)
    return {
        "gradient": draw_gradient(jax.random.fold_in(splits[6], 71), 0),
        "block_slot": draw_block_slot(jax.random.fold_in(splits[6], 71), 0),
        "left_factor": draw_left_factor(jax.random.fold_in(splits[6], 71), 0),
        "right_factor": draw_right_factor(jax.random.fold_in(splits[6], 71), 0),
        "left_root": draw_left_root(jax.random.fold_in(splits[6], 71), 0),
        "right_root": draw_right_root(jax.random.fold_in(splits[6], 71), 0),
    }


def reference(gradient, block_slot, left_factor, right_factor, left_root, right_root):
    group_size = B * N_DP // D
    per_owner = N_TENSOR // group_size
    highest = lax.Precision.HIGHEST

    def one_block(block_index, state_carry):
        update, new_left, new_right = state_carry
        block_index = jnp.asarray(block_index).astype(jnp.int32)
        device = block_index // per_owner
        owner_local = block_index % per_owner
        row_device = device // N_TENSOR
        column_owner = device % N_TENSOR
        row_block = row_device // group_size
        position = row_device % group_size * per_owner + owner_local
        source = block_slot[row_block, column_owner, position].astype(jnp.int32)
        column_block = source * N_TENSOR + column_owner
        row_start = (row_block * B).astype(jnp.int32)
        col_start = (column_block * B).astype(jnp.int32)
        blocks = lax.dynamic_slice(gradient, (row_start, col_start), (B, B)).astype(jnp.float32)
        left_term = jnp.dot(blocks, blocks.T, precision=highest)
        right_term = jnp.dot(blocks.T, blocks, precision=highest)
        new_left = new_left.at[block_index].set(left_factor[block_index] + left_term)
        new_right = new_right.at[block_index].set(right_factor[block_index] + right_term)
        half_product = jnp.dot(left_root[block_index].astype(jnp.float32), blocks, precision=highest).astype(jnp.bfloat16)
        preconditioned = jnp.dot(half_product.astype(jnp.float32), right_root[block_index].astype(jnp.float32), precision=highest)
        graft_scale = jnp.sqrt(jnp.mean(blocks * blocks) / (jnp.mean(preconditioned * preconditioned) + 1e-06))
        update_piece = (graft_scale * preconditioned).astype(jnp.bfloat16)
        update = lax.dynamic_update_slice(update, update_piece, (row_start, col_start))
        return (update, new_left, new_right)
    start = (jnp.zeros((D, COLS), jnp.bfloat16), jnp.zeros_like(left_factor), jnp.zeros_like(right_factor))
    update, new_left, new_right = lax.fori_loop(0, BLOCKS, one_block, start)
    return (update, new_left, new_right)
```

```python
import jax
import jax.numpy as jnp
from jax import lax
from jax.experimental import pallas as pl
from jax.experimental.pallas import tpu as pltpu
from jax.sharding import PartitionSpec as P

B = 1024
GROUP = 4
TENSORS = 4
ROWS = B // GROUP
W = 128
CHUNKS = B // W
PANEL = 256
AHEAD = 3
MESH = pl.DeviceIdType.MESH


def fold(x):
    return jnp.sum(x.reshape(-1, 8, 128), axis=0)


def kernel(slot, grad, lf, rf, lroot, rroot, upd, nl, nr, *scratch):
    scratch = list(scratch)
    take = lambda n: [scratch.pop(0) for _ in range(n)]
    zr, yst, yr, zst = take(CHUNKS), take(CHUNKS), take(CHUNKS), take(CHUNKS)
    g, gt, half, pst, lv, rv, gsq, psq, sc_out, sc_in = take(10)
    load_sem, own_sem, z_send, z_recv, y_send, y_recv = take(6)
    by_send, by_recv, sc_send, sc_recv, bz_send, bz_recv = take(6)

    dp, z = lax.axis_index("dp"), lax.axis_index("tensor")
    m = lax.rem(dp, GROUP)
    base = dp - m
    row_block = lax.div(dp, GROUP)
    z_peers = [lax.rem(z + o, TENSORS) for o in range(TENSORS)]
    m_peers = [lax.rem(m + o, GROUP) for o in range(GROUP)]
    z_dev = [(dp, t) for t in z_peers]
    m_dev = [(base + q, z) for q in m_peers]

    loads = [
        pltpu.make_async_copy(src, dst, load_sem.at[i])
        for i, (src, dst) in enumerate(
            [(lroot.at[0], lv), (rroot.at[0], rv), (lf.at[0], nl), (rf.at[0], nr)]
        )
    ]

    def own_copy(c):
        return pltpu.make_async_copy(
            grad.at[:, pl.ds(pl.multiple_of(z * B + c * W, W), W)], zr[c].at[z], own_sem.at[c]
        )

    def z_copy(c, o):
        return pltpu.make_async_remote_copy(
            src_ref=grad.at[:, pl.ds(pl.multiple_of(z_peers[o] * B + c * W, W), W)],
            dst_ref=zr[c].at[z],
            send_sem=z_send.at[c, o],
            recv_sem=z_recv.at[c, o],
            device_id=z_dev[o],
            device_id_type=MESH,
        )

    def y_copy(c, o):
        return pltpu.make_async_remote_copy(
            src_ref=yst[c].at[o - 1],
            dst_ref=g.at[pl.ds(pl.multiple_of(m * ROWS, ROWS), ROWS), pl.ds(c * W, W)],
            send_sem=y_send.at[c, o],
            recv_sem=y_recv.at[c, o],
            device_id=m_dev[o],
            device_id_type=MESH,
        )

    def by_copy(c, o):
        return pltpu.make_async_remote_copy(
            src_ref=pst.at[pl.ds(pl.multiple_of(m_peers[o] * ROWS, ROWS), ROWS), pl.ds(c * W, W)],
            dst_ref=yr[c].at[m],
            send_sem=by_send.at[c, o],
            recv_sem=by_recv.at[c, o],
            device_id=m_dev[o],
            device_id_type=MESH,
        )

    def sc_copy(o):
        return pltpu.make_async_remote_copy(
            src_ref=sc_out,
            dst_ref=sc_in.at[m],
            send_sem=sc_send.at[o],
            recv_sem=sc_recv.at[o],
            device_id=m_dev[o],
            device_id_type=MESH,
        )

    def bz_copy(c, o):
        return pltpu.make_async_remote_copy(
            src_ref=zst[c].at[o - 1],
            dst_ref=upd.at[z, :, pl.ds(c * W, W)],
            send_sem=bz_send.at[c, o],
            recv_sem=bz_recv.at[c, o],
            device_id=z_dev[o],
            device_id_type=MESH,
        )

    others = (1, 3, 2)

    def send_z(c):
        for o in others:
            z_copy(c, o).start()
        own_copy(c).start()

    barrier = pltpu.get_barrier_semaphore()
    for o in range(1, TENSORS):
        pl.semaphore_signal(barrier, inc=1, device_id=z_dev[o], device_id_type=MESH)
    for o in range(1, GROUP):
        pl.semaphore_signal(barrier, inc=1, device_id=m_dev[o], device_id_type=MESH)
    pl.semaphore_wait(barrier, TENSORS + GROUP - 2)

    for c in range(AHEAD):
        send_z(c)
    for copy in loads:
        copy.start()

    gsq[...] = jnp.zeros_like(gsq)
    psq[...] = jnp.zeros_like(psq)
    mine = pl.ds(pl.multiple_of(m * ROWS, ROWS), ROWS)

    def relay(c):
        own_copy(c).wait()
        for o in others:
            z_copy(c, o).wait_recv()
        for o in (1, 2, 3):
            yst[c][o - 1] = zr[c][slot[row_block, z, m_peers[o]]]
            y_copy(c, o).start()
        g[mine, pl.ds(c * W, W)] = zr[c][slot[row_block, z, m]]

    def left_product(c):
        for o in (1, 2, 3):
            y_copy(c, o).wait_recv()
        cols = pl.ds(c * W, W)

        @pl.loop(0, B, step=PANEL)
        def _(r):
            rows = pl.ds(pl.multiple_of(r, PANEL), PANEL)
            part = g[rows, cols].astype(jnp.float32)
            gsq[...] += fold(part * part)
            half[rows, cols] = jnp.dot(
                lv[rows, :], g[:, cols], preferred_element_type=jnp.float32
            ).astype(jnp.bfloat16)

    for c in range(CHUNKS):
        relay(c)
        if c + AHEAD < CHUNKS:
            send_z(c + AHEAD)
        if c == 1:
            loads[0].wait()
        if c >= 2:
            left_product(c - 2)
    loads[1].wait()
    left_product(CHUNKS - 2)
    left_product(CHUNKS - 1)

    def right_product(p):
        cols = pl.ds(p * PANEL, PANEL)

        @pl.loop(0, B, step=PANEL)
        def _(r):
            rows = pl.ds(pl.multiple_of(r, PANEL), PANEL)
            part = jnp.dot(half[rows, :], rv[:, cols], preferred_element_type=jnp.float32)
            square = part * part
            psq[...] += fold(square[:, :128]) + fold(square[:, 128:])
            pst[rows, cols] = part.astype(jnp.bfloat16)

    def send_back(c):
        for o in (1, 2, 3):
            by_copy(c, o).start()
        yr[c][m] = pst[mine, pl.ds(c * W, W)]

    right_product(0)
    send_back(0)
    for p in range(1, B // PANEL):
        right_product(p)
    count = 1.0 / (B * B)
    grad_mean = jnp.sum(gsq[...], axis=(0, 1), keepdims=True) * count
    pre_mean = jnp.sum(psq[...], axis=(0, 1), keepdims=True) * count
    scale = jnp.broadcast_to(jnp.sqrt(grad_mean / (pre_mean + 1e-6)), (8, 128))
    sc_out[...] = scale
    sc_in[m] = scale
    for o in (1, 2, 3):
        sc_copy(o).start()
    for c in range(1, CHUNKS):
        send_back(c)

    def left_gram(p):
        cols = pl.ds(p * PANEL, PANEL)

        @pl.loop(0, B, step=PANEL)
        def _(r):
            rows = pl.ds(pl.multiple_of(r, PANEL), PANEL)
            nl[rows, cols] += lax.dot_general(
                g[rows, :], g[cols, :], (((1,), (1,)), ((), ())), preferred_element_type=jnp.float32
            )

    def right_gram(p):
        cols = pl.ds(p * PANEL, PANEL)

        @pl.loop(0, B, step=PANEL)
        def _(r):
            rows = pl.ds(pl.multiple_of(r, PANEL), PANEL)
            nr[rows, cols] += jnp.dot(gt[rows, :], g[:, cols], preferred_element_type=jnp.float32)

    loads[2].wait()
    loads[3].wait()

    @pl.loop(0, B, step=PANEL)
    def _(r):
        rows = pl.ds(pl.multiple_of(r, PANEL), PANEL)
        gt[rows, :] = g[:, rows].T

    slots = [slot[row_block, z, q] for q in range(GROUP)]

    def relay_back(c):
        for o in (1, 2, 3):
            by_copy(c, o).wait_recv()
        for o in (1, 3, 2, 0):
            t = z_peers[o]
            q = jnp.int32(0)
            for other in range(1, GROUP):
                q = jnp.where(slots[other] == t, other, q)
            piece = (yr[c][q].astype(jnp.float32) * sc_in[q][0:1, :]).astype(jnp.bfloat16)
            if o:
                zst[c][o - 1] = piece
                bz_copy(c, o).start()
            else:
                upd[z, :, pl.ds(c * W, W)] = piece

    for c in range(CHUNKS):
        if c == 0:
            for o in (1, 2, 3):
                sc_copy(o).wait_recv()
        relay_back(c)
        if c < 4:
            left_gram(c)
        else:
            right_gram(c - 4)

    for c in range(CHUNKS):
        for o in (1, 2, 3):
            z_copy(c, o).wait_send()
            y_copy(c, o).wait_send()
            by_copy(c, o).wait_send()
            bz_copy(c, o).wait_send()
    for o in (1, 2, 3):
        sc_copy(o).wait_send()
    for c in range(CHUNKS):
        for o in (1, 2, 3):
            bz_copy(c, o).wait_recv()


def write_out(upd, nl, nr, update, new_left, new_right, sem):
    copies = [
        (upd.at[e], update.at[:, pl.ds(e * B, B)]) for e in range(TENSORS)
    ]
    for i in range(4):
        rows = pl.ds(i * ROWS, ROWS)
        copies.append((nl.at[rows], new_left.at[0, rows]))
        copies.append((nr.at[rows], new_right.at[0, rows]))
    copies = [pltpu.make_async_copy(a, b, sem.at[i]) for i, (a, b) in enumerate(copies)]
    for copy in copies:
        copy.start()
    for copy in copies:
        copy.wait()


def per_device(gradient, block_slot, left_factor, right_factor, left_root, right_root):
    vmem, hbm = pl.BlockSpec(memory_space=pltpu.VMEM), pl.BlockSpec(memory_space=pltpu.HBM)
    smem = pl.BlockSpec(memory_space=pltpu.SMEM)
    bf16, f32 = jnp.bfloat16, jnp.float32
    dma = pltpu.SemaphoreType.DMA
    parts = pl.pallas_call(
        kernel,
        out_shape=(
            pltpu.VMEM((TENSORS, ROWS, B), bf16),
            pltpu.VMEM((B, B), f32),
            pltpu.VMEM((B, B), f32),
        ),
        in_specs=[smem, hbm, hbm, hbm, hbm, hbm],
        out_specs=(vmem, vmem, vmem),
        scratch_shapes=[pltpu.VMEM((4, ROWS, W), bf16)] * CHUNKS
        + [pltpu.VMEM((3, ROWS, W), bf16)] * CHUNKS
        + [pltpu.VMEM((4, ROWS, W), bf16)] * CHUNKS
        + [pltpu.VMEM((3, ROWS, W), bf16)] * CHUNKS
        + [pltpu.VMEM((B, B), bf16)] * 6
        + [pltpu.VMEM((8, 128), f32)] * 3
        + [pltpu.VMEM((4, 8, 128), f32)]
        + [dma((4,)), dma((CHUNKS,))]
        + [dma((CHUNKS, 4))] * 6
        + [dma((4,))] * 2
        + [dma((CHUNKS, 4))] * 2,
        compiler_params=pltpu.CompilerParams(
            collective_id=0, has_side_effects=True, vmem_limit_bytes=32 * 2**20
        ),
        name="shampoo",
    )(
        block_slot,
        *[
            pltpu.with_memory_space_constraint(x, pltpu.HBM)
            for x in (gradient, left_factor, right_factor, left_root, right_root)
        ],
    )
    return pl.pallas_call(
        write_out,
        out_shape=(
            pltpu.HBM((ROWS, TENSORS * B), bf16),
            pltpu.HBM((1, B, B), f32),
            pltpu.HBM((1, B, B), f32),
        ),
        in_specs=[vmem] * 3,
        out_specs=[hbm] * 3,
        scratch_shapes=[dma((12,))],
        compiler_params=pltpu.CompilerParams(vmem_limit_bytes=2**20),
        name="write_out",
    )(*[pltpu.with_memory_space_constraint(x, pltpu.VMEM) for x in parts])


def solution(mesh):
    owned = P(("dp", "tensor"), None, None)
    return jax.shard_map(
        per_device,
        mesh=mesh,
        in_specs=(P("dp", "tensor"), P(), owned, owned, owned, owned),
        out_specs=(P("dp", "tensor"), owned, owned),
        check_vma=False,
    )
```

```python
import jax
import jax.numpy as jnp
from jax import lax
from jax.experimental import pallas as pl
from jax.experimental.pallas import tpu as pltpu
from jax.sharding import PartitionSpec as P

B = 1024
GROUP = 4
TENSORS = 4
ROWS = B // GROUP
W = 128
CHUNKS = B // W
PANEL = 256
AHEAD = 3
MESH = pl.DeviceIdType.MESH


def fold(x):
    return jnp.sum(x.reshape(-1, 8, 128), axis=0)


def kernel(slot_hbm, grad, lf, rf, lroot, rroot, upd, nl, nr, *scratch):
    scratch = list(scratch)
    take = lambda n: [scratch.pop(0) for _ in range(n)]
    zr, yst, yr, zst = take(CHUNKS), take(CHUNKS), take(CHUNKS), take(CHUNKS)
    g, gt, half, pst, lv, rv, gsq, psq, sc_out, sc_in = take(10)
    slot, slot_sem, acc = take(3)
    load_sem, own_sem, z_send, z_recv, y_send, y_recv = take(6)
    by_send, by_recv, sc_send, sc_recv, bz_send, bz_recv = take(6)

    dp, z = lax.axis_index("dp"), lax.axis_index("tensor")
    m = lax.rem(dp, GROUP)
    base = dp - m
    row_block = lax.div(dp, GROUP)
    z_peers = [lax.rem(z + o, TENSORS) for o in range(TENSORS)]
    m_peers = [lax.rem(m + o, GROUP) for o in range(GROUP)]
    z_dev = [(dp, t) for t in z_peers]
    m_dev = [(base + q, z) for q in m_peers]

    loads = [
        pltpu.make_async_copy(src, dst, load_sem.at[i])
        for i, (src, dst) in enumerate(
            [(lroot.at[0], lv), (rroot.at[0], rv), (lf.at[0], nl), (rf.at[0], nr)]
        )
    ]

    def own_copy(c):
        return pltpu.make_async_copy(
            grad.at[:, pl.ds(pl.multiple_of(z * B + c * W, W), W)], zr[c].at[z], own_sem.at[c]
        )

    def z_copy(c, o):
        return pltpu.make_async_remote_copy(
            src_ref=grad.at[:, pl.ds(pl.multiple_of(z_peers[o] * B + c * W, W), W)],
            dst_ref=zr[c].at[z],
            send_sem=z_send.at[c, o],
            recv_sem=z_recv.at[c, o],
            device_id=z_dev[o],
            device_id_type=MESH,
        )

    def y_copy(c, o):
        return pltpu.make_async_remote_copy(
            src_ref=yst[c].at[o - 1],
            dst_ref=g.at[pl.ds(pl.multiple_of(m * ROWS, ROWS), ROWS), pl.ds(c * W, W)],
            send_sem=y_send.at[c, o],
            recv_sem=y_recv.at[c, o],
            device_id=m_dev[o],
            device_id_type=MESH,
        )

    def by_copy(c, o):
        return pltpu.make_async_remote_copy(
            src_ref=pst.at[pl.ds(pl.multiple_of(m_peers[o] * ROWS, ROWS), ROWS), pl.ds(c * W, W)],
            dst_ref=yr[c].at[m],
            send_sem=by_send.at[c, o],
            recv_sem=by_recv.at[c, o],
            device_id=m_dev[o],
            device_id_type=MESH,
        )

    def sc_copy(o):
        return pltpu.make_async_remote_copy(
            src_ref=sc_out,
            dst_ref=sc_in.at[m],
            send_sem=sc_send.at[o],
            recv_sem=sc_recv.at[o],
            device_id=m_dev[o],
            device_id_type=MESH,
        )

    def bz_copy(c, o):
        return pltpu.make_async_remote_copy(
            src_ref=zst[c].at[o - 1],
            dst_ref=upd.at[z, :, pl.ds(c * W, W)],
            send_sem=bz_send.at[c, o],
            recv_sem=bz_recv.at[c, o],
            device_id=z_dev[o],
            device_id_type=MESH,
        )

    others = (2, 1, 3)

    def send_z(c):
        for o in others:
            z_copy(c, o).start()
        own_copy(c).start()

    slot_copy = pltpu.make_async_copy(slot_hbm, slot, slot_sem)
    slot_copy.start()
    barrier = pltpu.get_barrier_semaphore()
    for o in range(1, TENSORS):
        pl.semaphore_signal(barrier, inc=1, device_id=z_dev[o], device_id_type=MESH)
    for o in range(1, GROUP):
        pl.semaphore_signal(barrier, inc=1, device_id=m_dev[o], device_id_type=MESH)
    pl.semaphore_wait(barrier, TENSORS + GROUP - 2)

    for c in range(AHEAD):
        send_z(c)
    for copy in loads:
        copy.start()
    slot_copy.wait()

    gsq[...] = jnp.zeros_like(gsq)
    psq[...] = jnp.zeros_like(psq)
    mine = pl.ds(pl.multiple_of(m * ROWS, ROWS), ROWS)

    def relay(c):
        own_copy(c).wait()
        for o in others:
            z_copy(c, o).wait_recv()
        for o in (1, 2, 3):
            yst[c][o - 1] = zr[c][slot[z, m_peers[o], row_block]]
            y_copy(c, o).start()
        g[mine, pl.ds(c * W, W)] = zr[c][slot[z, m, row_block]]

    def left_product(c):
        for o in (1, 2, 3):
            y_copy(c, o).wait_recv()
        cols = pl.ds(c * W, W)

        @pl.loop(0, B, step=PANEL, unroll=True)
        def _(r):
            rows = pl.ds(pl.multiple_of(r, PANEL), PANEL)
            part = g[rows, cols].astype(jnp.float32)
            gsq[...] += fold(part * part)
            half[rows, cols] = jnp.dot(
                lv[rows, :], g[:, cols], preferred_element_type=jnp.float32
            ).astype(jnp.bfloat16)

    def partial_right(start, stop):
        inner = pl.ds(start * W, (stop - start) * W)

        @pl.loop(0, B, step=PANEL, unroll=True)
        def _(r):
            rows = pl.ds(pl.multiple_of(r, PANEL), PANEL)
            part = jnp.dot(half[rows, inner], rv[inner, :], preferred_element_type=jnp.float32)
            acc[rows, :] = part if start == 0 else acc[rows, :] + part

    for c in range(CHUNKS):
        relay(c)
        if c + AHEAD < CHUNKS:
            send_z(c + AHEAD)
        if c == 1:
            loads[0].wait()
        if c >= 2:
            left_product(c - 2)
        if c == 4:
            loads[1].wait()
            partial_right(0, 2)
        if c == 6:
            partial_right(2, 4)
    partial_right(4, 6)
    left_product(CHUNKS - 2)
    partial_right(6, 7)
    left_product(CHUNKS - 1)

    inner = pl.ds(7 * W, W)

    def right_product(p):
        cols = pl.ds(p * PANEL, PANEL)

        @pl.loop(0, B, step=PANEL, unroll=True)
        def _(r):
            rows = pl.ds(pl.multiple_of(r, PANEL), PANEL)
            part = acc[rows, cols] + jnp.dot(
                half[rows, inner], rv[inner, cols], preferred_element_type=jnp.float32
            )
            square = part * part
            psq[...] += fold(square[:, :128]) + fold(square[:, 128:])
            pst[rows, cols] = part.astype(jnp.bfloat16)

    def send_back(c):
        for o in (1, 2, 3):
            by_copy(c, o).start()
        yr[c][m] = pst[mine, pl.ds(c * W, W)]

    right_product(0)
    send_back(0)
    for p in range(1, B // PANEL):
        right_product(p)
    count = 1.0 / (B * B)
    grad_mean = jnp.sum(gsq[...], axis=(0, 1), keepdims=True) * count
    pre_mean = jnp.sum(psq[...], axis=(0, 1), keepdims=True) * count
    scale = jnp.broadcast_to(jnp.sqrt(grad_mean / (pre_mean + 1e-6)), (8, 128))
    sc_out[...] = scale
    sc_in[m] = scale
    for o in (1, 2, 3):
        sc_copy(o).start()
    for c in range(1, CHUNKS):
        send_back(c)

    def left_gram(p):
        cols = pl.ds(p * PANEL, PANEL)

        @pl.loop(0, B, step=PANEL, unroll=True)
        def _(r):
            rows = pl.ds(pl.multiple_of(r, PANEL), PANEL)
            nl[rows, cols] += lax.dot_general(
                g[rows, :], g[cols, :], (((1,), (1,)), ((), ())), preferred_element_type=jnp.float32
            )

    def right_gram(p):
        cols = pl.ds(p * PANEL, PANEL)

        @pl.loop(0, B, step=PANEL, unroll=True)
        def _(r):
            rows = pl.ds(pl.multiple_of(r, PANEL), PANEL)
            nr[rows, cols] += jnp.dot(gt[rows, :], g[:, cols], preferred_element_type=jnp.float32)

    loads[2].wait()
    loads[3].wait()

    @pl.loop(0, B, step=PANEL, unroll=True)
    def _(r):
        rows = pl.ds(pl.multiple_of(r, PANEL), PANEL)
        gt[rows, :] = g[:, rows].T

    slots = [slot[z, q, row_block] for q in range(GROUP)]

    def relay_back(c):
        for o in (1, 2, 3):
            by_copy(c, o).wait_recv()
        for o in (2, 1, 3, 0):
            t = z_peers[o]
            q = jnp.int32(0)
            for other in range(1, GROUP):
                q = jnp.where(slots[other] == t, other, q)
            piece = (yr[c][q].astype(jnp.float32) * sc_in[q][0:1, :]).astype(jnp.bfloat16)
            if o:
                zst[c][o - 1] = piece
                bz_copy(c, o).start()
            else:
                upd[z, :, pl.ds(c * W, W)] = piece

    for o in (1, 2, 3):
        sc_copy(o).wait_recv()
    for c in range(CHUNKS):
        relay_back(c)
        if c < 4:
            left_gram(c)
        else:
            right_gram(c - 4)
        for o in (1, 2, 3):
            z_copy(c, o).wait_send()
            y_copy(c, o).wait_send()
            if c:
                by_copy(c - 1, o).wait_send()
    for o in (1, 2, 3):
        sc_copy(o).wait_send()
        by_copy(CHUNKS - 1, o).wait_send()
    for c in range(CHUNKS):
        for o in (1, 2, 3):
            bz_copy(c, o).wait()


def write_out(upd, nl, nr, update, new_left, new_right, sem):
    copies = [
        (upd.at[e], update.at[:, pl.ds(e * B, B)]) for e in range(TENSORS)
    ]
    for i in range(4):
        rows = pl.ds(i * ROWS, ROWS)
        copies.append((nl.at[rows], new_left.at[0, rows]))
        copies.append((nr.at[rows], new_right.at[0, rows]))
    copies = [pltpu.make_async_copy(a, b, sem.at[i]) for i, (a, b) in enumerate(copies)]
    for copy in copies:
        copy.start()
    for copy in copies:
        copy.wait()


def per_device(gradient, block_slot, left_factor, right_factor, left_root, right_root):
    vmem, hbm = pl.BlockSpec(memory_space=pltpu.VMEM), pl.BlockSpec(memory_space=pltpu.HBM)
    bf16, f32 = jnp.bfloat16, jnp.float32
    dma = pltpu.SemaphoreType.DMA
    parts = pl.pallas_call(
        kernel,
        out_shape=(
            pltpu.VMEM((TENSORS, ROWS, B), bf16),
            pltpu.VMEM((B, B), f32),
            pltpu.VMEM((B, B), f32),
        ),
        in_specs=[hbm, hbm, hbm, hbm, hbm, hbm],
        out_specs=(vmem, vmem, vmem),
        scratch_shapes=[pltpu.VMEM((4, ROWS, W), bf16)] * CHUNKS
        + [pltpu.VMEM((3, ROWS, W), bf16)] * CHUNKS
        + [pltpu.VMEM((4, ROWS, W), bf16)] * CHUNKS
        + [pltpu.VMEM((3, ROWS, W), bf16)] * CHUNKS
        + [pltpu.VMEM((B, B), bf16)] * 6
        + [pltpu.VMEM((8, 128), f32)] * 3
        + [pltpu.VMEM((4, 8, 128), f32)]
        + [pltpu.SMEM((TENSORS, GROUP, block_slot.shape[0]), jnp.int32), dma]
        + [pltpu.VMEM((B, B), f32)]
        + [dma((4,)), dma((CHUNKS,))]
        + [dma((CHUNKS, 4))] * 6
        + [dma((4,))] * 2
        + [dma((CHUNKS, 4))] * 2,
        compiler_params=pltpu.CompilerParams(
            collective_id=0, has_side_effects=True, vmem_limit_bytes=32 * 2**20
        ),
        name="shampoo",
    )(
        *[
            pltpu.with_memory_space_constraint(x, pltpu.HBM)
            for x in (block_slot.transpose(1, 2, 0), gradient, left_factor, right_factor, left_root, right_root)
        ],
    )
    return pl.pallas_call(
        write_out,
        out_shape=(
            pltpu.HBM((ROWS, TENSORS * B), bf16),
            pltpu.HBM((1, B, B), f32),
            pltpu.HBM((1, B, B), f32),
        ),
        in_specs=[vmem] * 3,
        out_specs=[hbm] * 3,
        scratch_shapes=[dma((12,))],
        compiler_params=pltpu.CompilerParams(vmem_limit_bytes=2**20),
        name="write_out",
    )(*[pltpu.with_memory_space_constraint(x, pltpu.VMEM) for x in parts])


def solution(mesh):
    owned = P(("dp", "tensor"), None, None)
    return jax.shard_map(
        per_device,
        mesh=mesh,
        in_specs=(P("dp", "tensor"), P(), owned, owned, owned, owned),
        out_specs=(P("dp", "tensor"), owned, owned),
        check_vma=False,
    )
```

```python
import jax
import jax.numpy as jnp
from jax import lax
from jax.experimental import pallas as pl
from jax.experimental.pallas import tpu as pltpu
from jax.sharding import PartitionSpec as P

B = 1024
GROUP = 4
TENSORS = 4
ROWS = B // GROUP
W = 128
CHUNKS = B // W
HALVES = 1
PART = ROWS // HALVES
STEPS = CHUNKS * HALVES
PANEL = 256
AHEAD = 3
MESH = pl.DeviceIdType.MESH


def fold(x):
    return jnp.sum(x.reshape(-1, 8, 128), axis=0)


def kernel(slot_hbm, grad, lf, rf, lroot, rroot, upd, nl, nr, *scratch):
    scratch = list(scratch)
    take = lambda n: [scratch.pop(0) for _ in range(n)]
    zr, yst, yr, zst = take(STEPS), take(STEPS), take(STEPS), take(STEPS)
    g, gt, half, pst, lv, rv, gsq, psq, sc_out, sc_in = take(10)
    slot, slot_sem, acc = take(3)
    load_sem, own_sem, z_send, z_recv, y_send, y_recv = take(6)
    by_send, by_recv, sc_send, sc_recv, bz_send, bz_recv = take(6)

    dp, z = lax.axis_index("dp"), lax.axis_index("tensor")
    m = lax.rem(dp, GROUP)
    base = dp - m
    row_block = lax.div(dp, GROUP)
    z_peers = [lax.rem(z + o, TENSORS) for o in range(TENSORS)]
    m_peers = [lax.rem(m + o, GROUP) for o in range(GROUP)]
    z_dev = [(dp, t) for t in z_peers]
    m_dev = [(base + q, z) for q in m_peers]

    loads = [
        pltpu.make_async_copy(src, dst, load_sem.at[i])
        for i, (src, dst) in enumerate(
            [(lroot.at[0], lv), (rroot.at[0], rv), (lf.at[0], nl), (rf.at[0], nr)]
        )
    ]

    def part_rows(c):
        return pl.ds(c % HALVES * PART, PART)

    def block_rows(q, c):
        return pl.ds(pl.multiple_of(q * ROWS + c % HALVES * PART, PART), PART)

    def part_cols(c):
        return pl.ds(c // HALVES * W, W)

    def own_copy(c):
        return pltpu.make_async_copy(
            grad.at[part_rows(c), pl.ds(pl.multiple_of(z * B + c // HALVES * W, W), W)],
            zr[c].at[z],
            own_sem.at[c],
        )

    def z_copy(c, o):
        return pltpu.make_async_remote_copy(
            src_ref=grad.at[
                part_rows(c), pl.ds(pl.multiple_of(z_peers[o] * B + c // HALVES * W, W), W)
            ],
            dst_ref=zr[c].at[z],
            send_sem=z_send.at[c, o],
            recv_sem=z_recv.at[c, o],
            device_id=z_dev[o],
            device_id_type=MESH,
        )

    def y_copy(c, o):
        return pltpu.make_async_remote_copy(
            src_ref=yst[c].at[o - 1],
            dst_ref=g.at[block_rows(m, c), part_cols(c)],
            send_sem=y_send.at[c, o],
            recv_sem=y_recv.at[c, o],
            device_id=m_dev[o],
            device_id_type=MESH,
        )

    def by_copy(c, o):
        return pltpu.make_async_remote_copy(
            src_ref=pst.at[block_rows(m_peers[o], c), part_cols(c)],
            dst_ref=yr[c].at[m],
            send_sem=by_send.at[c, o],
            recv_sem=by_recv.at[c, o],
            device_id=m_dev[o],
            device_id_type=MESH,
        )

    def sc_copy(o):
        return pltpu.make_async_remote_copy(
            src_ref=sc_out,
            dst_ref=sc_in.at[m],
            send_sem=sc_send.at[o],
            recv_sem=sc_recv.at[o],
            device_id=m_dev[o],
            device_id_type=MESH,
        )

    def bz_copy(c, o):
        return pltpu.make_async_remote_copy(
            src_ref=zst[c].at[o - 1],
            dst_ref=upd.at[z, part_rows(c), part_cols(c)],
            send_sem=bz_send.at[c, o],
            recv_sem=bz_recv.at[c, o],
            device_id=z_dev[o],
            device_id_type=MESH,
        )

    others = (2, 1, 3)

    def send_z(c):
        for o in others:
            z_copy(c, o).start()
        own_copy(c).start()

    slot_copy = pltpu.make_async_copy(slot_hbm, slot, slot_sem)
    slot_copy.start()
    barrier = pltpu.get_barrier_semaphore()
    for o in range(1, TENSORS):
        pl.semaphore_signal(barrier, inc=1, device_id=z_dev[o], device_id_type=MESH)
    for o in range(1, GROUP):
        pl.semaphore_signal(barrier, inc=1, device_id=m_dev[o], device_id_type=MESH)
    pl.semaphore_wait(barrier, TENSORS + GROUP - 2)

    for c in range(AHEAD):
        send_z(c)
    for copy in loads:
        copy.start()
    slot_copy.wait()

    gsq[...] = jnp.zeros_like(gsq)
    psq[...] = jnp.zeros_like(psq)

    def relay(c):
        own_copy(c).wait()
        for o in others:
            z_copy(c, o).wait_recv()
        for o in (1, 2, 3):
            yst[c][o - 1] = zr[c][slot[z, m_peers[o], row_block]]
            y_copy(c, o).start()
        g[block_rows(m, c), part_cols(c)] = zr[c][slot[z, m, row_block]]

    def left_product(c):
        for h in range(HALVES):
            for o in (1, 2, 3):
                y_copy(c * HALVES + h, o).wait_recv()
        cols = pl.ds(c * W, W)

        @pl.loop(0, B, step=PANEL, unroll=True)
        def _(r):
            rows = pl.ds(pl.multiple_of(r, PANEL), PANEL)
            part = g[rows, cols].astype(jnp.float32)
            gsq[...] += fold(part * part)
            half[rows, cols] = jnp.dot(
                lv[rows, :], g[:, cols], preferred_element_type=jnp.float32
            ).astype(jnp.bfloat16)

    def partial_right(start, stop):
        inner = pl.ds(start * W, (stop - start) * W)

        @pl.loop(0, B, step=PANEL, unroll=True)
        def _(r):
            rows = pl.ds(pl.multiple_of(r, PANEL), PANEL)
            part = jnp.dot(half[rows, inner], rv[inner, :], preferred_element_type=jnp.float32)
            acc[rows, :] = part if start == 0 else acc[rows, :] + part

    for c in range(CHUNKS):
        for k in range(c * HALVES, (c + 1) * HALVES):
            relay(k)
            if k + AHEAD < STEPS:
                send_z(k + AHEAD)
        if c == 1:
            loads[0].wait()
        if c >= 2:
            left_product(c - 2)
        if c == 4:
            loads[1].wait()
            partial_right(0, 2)
        if c == 6:
            partial_right(2, 4)
    partial_right(4, 6)
    left_product(CHUNKS - 2)
    partial_right(6, 7)
    left_product(CHUNKS - 1)

    inner = pl.ds(7 * W, W)

    def right_product(start, width):
        cols = pl.ds(start, width)

        @pl.loop(0, B, step=PANEL, unroll=True)
        def _(r):
            rows = pl.ds(pl.multiple_of(r, PANEL), PANEL)
            part = acc[rows, cols] + jnp.dot(
                half[rows, inner], rv[inner, cols], preferred_element_type=jnp.float32
            )
            square = part * part
            for j in range(0, width, 128):
                psq[...] += fold(square[:, j : j + 128])
            pst[rows, cols] = part.astype(jnp.bfloat16)

    def send_back(c):
        for o in (1, 2, 3):
            by_copy(c, o).start()
        yr[c][m] = pst[block_rows(m, c), part_cols(c)]

    right_product(0, W)
    for k in range(HALVES):
        send_back(k)
    right_product(W, W)
    for p in range(1, B // PANEL):
        right_product(p * PANEL, PANEL)
    count = 1.0 / (B * B)
    grad_mean = jnp.sum(gsq[...], axis=(0, 1), keepdims=True) * count
    pre_mean = jnp.sum(psq[...], axis=(0, 1), keepdims=True) * count
    scale = jnp.broadcast_to(jnp.sqrt(grad_mean / (pre_mean + 1e-6)), (8, 128))
    sc_out[...] = scale
    sc_in[m] = scale
    for o in (1, 2, 3):
        sc_copy(o).start()
    for k in range(HALVES, STEPS):
        send_back(k)

    def left_gram(p):
        cols = pl.ds(p * PANEL, PANEL)

        @pl.loop(0, B, step=PANEL, unroll=True)
        def _(r):
            rows = pl.ds(pl.multiple_of(r, PANEL), PANEL)
            nl[rows, cols] += lax.dot_general(
                g[rows, :], g[cols, :], (((1,), (1,)), ((), ())), preferred_element_type=jnp.float32
            )

    def right_gram(p):
        cols = pl.ds(p * PANEL, PANEL)

        @pl.loop(0, B, step=PANEL, unroll=True)
        def _(r):
            rows = pl.ds(pl.multiple_of(r, PANEL), PANEL)
            nr[rows, cols] += jnp.dot(gt[rows, :], g[:, cols], preferred_element_type=jnp.float32)

    loads[2].wait()
    loads[3].wait()

    @pl.loop(0, B, step=PANEL, unroll=True)
    def _(r):
        rows = pl.ds(pl.multiple_of(r, PANEL), PANEL)
        gt[rows, :] = g[:, rows].T

    slots = [slot[z, q, row_block] for q in range(GROUP)]

    def relay_back(c):
        for o in (1, 2, 3):
            by_copy(c, o).wait_recv()
        for o in (2, 1, 3, 0):
            t = z_peers[o]
            q = jnp.int32(0)
            for other in range(1, GROUP):
                q = jnp.where(slots[other] == t, other, q)
            piece = (yr[c][q].astype(jnp.float32) * sc_in[q][0:1, :]).astype(jnp.bfloat16)
            if o:
                zst[c][o - 1] = piece
                bz_copy(c, o).start()
            else:
                upd[z, part_rows(c), part_cols(c)] = piece

    for o in (1, 2, 3):
        sc_copy(o).wait_recv()
    for k in range(STEPS):
        relay_back(k)
        if k < 4:
            left_gram(k)
        else:
            right_gram(k - 4)
        for o in (1, 2, 3):
            z_copy(k, o).wait_send()
            y_copy(k, o).wait_send()
            if k:
                by_copy(k - 1, o).wait_send()
    for o in (1, 2, 3):
        sc_copy(o).wait_send()
        by_copy(STEPS - 1, o).wait_send()
    for k in range(STEPS):
        for o in (1, 2, 3):
            bz_copy(k, o).wait()


def write_out(upd, nl, nr, update, new_left, new_right, sem):
    copies = [
        (upd.at[e], update.at[:, pl.ds(e * B, B)]) for e in range(TENSORS)
    ]
    for i in range(4):
        rows = pl.ds(i * ROWS, ROWS)
        copies.append((nl.at[rows], new_left.at[0, rows]))
        copies.append((nr.at[rows], new_right.at[0, rows]))
    copies = [pltpu.make_async_copy(a, b, sem.at[i]) for i, (a, b) in enumerate(copies)]
    for copy in copies:
        copy.start()
    for copy in copies:
        copy.wait()


def per_device(gradient, block_slot, left_factor, right_factor, left_root, right_root):
    vmem, hbm = pl.BlockSpec(memory_space=pltpu.VMEM), pl.BlockSpec(memory_space=pltpu.HBM)
    bf16, f32 = jnp.bfloat16, jnp.float32
    dma = pltpu.SemaphoreType.DMA
    parts = pl.pallas_call(
        kernel,
        out_shape=(
            pltpu.VMEM((TENSORS, ROWS, B), bf16),
            pltpu.VMEM((B, B), f32),
            pltpu.VMEM((B, B), f32),
        ),
        in_specs=[hbm, hbm, hbm, hbm, hbm, hbm],
        out_specs=(vmem, vmem, vmem),
        scratch_shapes=[pltpu.VMEM((4, PART, W), bf16)] * STEPS
        + [pltpu.VMEM((3, PART, W), bf16)] * STEPS
        + [pltpu.VMEM((4, PART, W), bf16)] * STEPS
        + [pltpu.VMEM((3, PART, W), bf16)] * STEPS
        + [pltpu.VMEM((B, B), bf16)] * 6
        + [pltpu.VMEM((8, 128), f32)] * 3
        + [pltpu.VMEM((4, 8, 128), f32)]
        + [pltpu.SMEM((TENSORS, GROUP, block_slot.shape[0]), jnp.int32), dma]
        + [pltpu.VMEM((B, B), f32)]
        + [dma((4,)), dma((STEPS,))]
        + [dma((STEPS, 4))] * 6
        + [dma((4,))] * 2
        + [dma((STEPS, 4))] * 2,
        compiler_params=pltpu.CompilerParams(
            collective_id=0, has_side_effects=True, vmem_limit_bytes=32 * 2**20
        ),
        name="shampoo",
    )(
        *[
            pltpu.with_memory_space_constraint(x, pltpu.HBM)
            for x in (block_slot.transpose(1, 2, 0), gradient, left_factor, right_factor, left_root, right_root)
        ],
    )
    return pl.pallas_call(
        write_out,
        out_shape=(
            pltpu.HBM((ROWS, TENSORS * B), bf16),
            pltpu.HBM((1, B, B), f32),
            pltpu.HBM((1, B, B), f32),
        ),
        in_specs=[vmem] * 3,
        out_specs=[hbm] * 3,
        scratch_shapes=[dma((12,))],
        compiler_params=pltpu.CompilerParams(vmem_limit_bytes=2**20),
        name="write_out",
    )(*[pltpu.with_memory_space_constraint(x, pltpu.VMEM) for x in parts])


def solution(mesh):
    owned = P(("dp", "tensor"), None, None)
    return jax.shard_map(
        per_device,
        mesh=mesh,
        in_specs=(P("dp", "tensor"), P(), owned, owned, owned, owned),
        out_specs=(P("dp", "tensor"), owned, owned),
        check_vma=False,
    )
```

```python
import jax
import jax.numpy as jnp
from jax import lax
from jax.experimental import pallas as pl
from jax.experimental.pallas import tpu as pltpu
from jax.sharding import PartitionSpec as P

B = 1024
GROUP = 4
TENSORS = 4
ROWS = B // GROUP
W = 128
CHUNKS = B // W
HALVES = 2
PART = ROWS // HALVES
STEPS = CHUNKS * HALVES
PANEL = 256
AHEAD = 6
MESH = pl.DeviceIdType.MESH


def fold(x):
    return jnp.sum(x.reshape(-1, 8, 128), axis=0)


def kernel(slot_hbm, grad, lf, rf, lroot, rroot, upd, nl, nr, *scratch):
    scratch = list(scratch)
    take = lambda n: [scratch.pop(0) for _ in range(n)]
    zr, yst, yr, zst = take(STEPS), take(STEPS), take(STEPS), take(STEPS)
    g, gt, half, pst, lv, rv, gsq, psq, sc_out, sc_in = take(10)
    slot, slot_sem, acc = take(3)
    load_sem, own_sem, z_send, z_recv, y_send, y_recv = take(6)
    by_send, by_recv, sc_send, sc_recv, bz_send, bz_recv = take(6)

    dp, z = lax.axis_index("dp"), lax.axis_index("tensor")
    m = lax.rem(dp, GROUP)
    base = dp - m
    row_block = lax.div(dp, GROUP)
    z_peers = [lax.rem(z + o, TENSORS) for o in range(TENSORS)]
    m_peers = [lax.rem(m + o, GROUP) for o in range(GROUP)]
    z_dev = [(dp, t) for t in z_peers]
    m_dev = [(base + q, z) for q in m_peers]

    loads = [
        pltpu.make_async_copy(src, dst, load_sem.at[i])
        for i, (src, dst) in enumerate(
            [(lroot.at[0], lv), (rroot.at[0], rv), (lf.at[0], nl), (rf.at[0], nr)]
        )
    ]

    def part_rows(c):
        return pl.ds(c % HALVES * PART, PART)

    def block_rows(q, c):
        return pl.ds(pl.multiple_of(q * ROWS + c % HALVES * PART, PART), PART)

    def part_cols(c):
        return pl.ds(c // HALVES * W, W)

    def own_copy(c):
        return pltpu.make_async_copy(
            grad.at[part_rows(c), pl.ds(pl.multiple_of(z * B + c // HALVES * W, W), W)],
            zr[c].at[z],
            own_sem.at[c],
        )

    def z_copy(c, o):
        return pltpu.make_async_remote_copy(
            src_ref=grad.at[
                part_rows(c), pl.ds(pl.multiple_of(z_peers[o] * B + c // HALVES * W, W), W)
            ],
            dst_ref=zr[c].at[z],
            send_sem=z_send.at[c, o - 1],
            recv_sem=z_recv.at[c, o - 1],
            device_id=z_dev[o],
            device_id_type=MESH,
        )

    def y_copy(c, o):
        return pltpu.make_async_remote_copy(
            src_ref=yst[c].at[o - 1],
            dst_ref=g.at[block_rows(m, c), part_cols(c)],
            send_sem=y_send.at[c, o - 1],
            recv_sem=y_recv.at[c, o - 1],
            device_id=m_dev[o],
            device_id_type=MESH,
        )

    def by_copy(c, o):
        return pltpu.make_async_remote_copy(
            src_ref=pst.at[block_rows(m_peers[o], c), part_cols(c)],
            dst_ref=yr[c].at[m],
            send_sem=by_send.at[c, o - 1],
            recv_sem=by_recv.at[c, o - 1],
            device_id=m_dev[o],
            device_id_type=MESH,
        )

    def sc_copy(o):
        return pltpu.make_async_remote_copy(
            src_ref=sc_out,
            dst_ref=sc_in.at[m],
            send_sem=sc_send.at[o],
            recv_sem=sc_recv.at[o],
            device_id=m_dev[o],
            device_id_type=MESH,
        )

    def bz_copy(c, o):
        return pltpu.make_async_remote_copy(
            src_ref=zst[c].at[o - 1],
            dst_ref=upd.at[z, part_rows(c), part_cols(c)],
            send_sem=bz_send.at[c, o - 1],
            recv_sem=bz_recv.at[c, o - 1],
            device_id=z_dev[o],
            device_id_type=MESH,
        )

    others = (2, 1, 3)

    def send_z(c):
        for o in others:
            z_copy(c, o).start()
        own_copy(c).start()

    slot_copy = pltpu.make_async_copy(slot_hbm, slot, slot_sem)
    slot_copy.start()
    barrier = pltpu.get_barrier_semaphore()
    for o in range(1, TENSORS):
        pl.semaphore_signal(barrier, inc=1, device_id=z_dev[o], device_id_type=MESH)
    for o in range(1, GROUP):
        pl.semaphore_signal(barrier, inc=1, device_id=m_dev[o], device_id_type=MESH)
    pl.semaphore_wait(barrier, TENSORS + GROUP - 2)

    for c in range(AHEAD):
        send_z(c)
    for copy in loads:
        copy.start()
    slot_copy.wait()

    gsq[...] = jnp.zeros_like(gsq)
    psq[...] = jnp.zeros_like(psq)

    def relay(c):
        own_copy(c).wait()
        for o in others:
            z_copy(c, o).wait_recv()
        for o in (1, 2, 3):
            yst[c][o - 1] = zr[c][slot[z, m_peers[o], row_block]]
            y_copy(c, o).start()
        g[block_rows(m, c), part_cols(c)] = zr[c][slot[z, m, row_block]]

    def left_product(c):
        for h in range(HALVES):
            for o in (1, 2, 3):
                y_copy(c * HALVES + h, o).wait_recv()
        cols = pl.ds(c * W, W)

        @pl.loop(0, B, step=PANEL, unroll=True)
        def _(r):
            rows = pl.ds(pl.multiple_of(r, PANEL), PANEL)
            part = g[rows, cols].astype(jnp.float32)
            gsq[...] += fold(part * part)
            half[rows, cols] = jnp.dot(
                lv[rows, :], g[:, cols], preferred_element_type=jnp.float32
            ).astype(jnp.bfloat16)

    def partial_right(start, stop):
        inner = pl.ds(start * W, (stop - start) * W)

        @pl.loop(0, B, step=PANEL, unroll=True)
        def _(r):
            rows = pl.ds(pl.multiple_of(r, PANEL), PANEL)
            part = jnp.dot(half[rows, inner], rv[inner, :], preferred_element_type=jnp.float32)
            acc[rows, :] = part if start == 0 else acc[rows, :] + part

    for c in range(CHUNKS):
        for k in range(c * HALVES, (c + 1) * HALVES):
            relay(k)
            if k + AHEAD < STEPS:
                send_z(k + AHEAD)
        if c == 1:
            loads[0].wait()
        if c >= 2:
            left_product(c - 2)
        if c == 4:
            loads[1].wait()
            partial_right(0, 2)
        if c == 6:
            partial_right(2, 4)
    partial_right(4, 6)
    left_product(CHUNKS - 2)
    partial_right(6, 7)
    left_product(CHUNKS - 1)

    inner = pl.ds(7 * W, W)

    def right_product(start, width):
        cols = pl.ds(start, width)

        @pl.loop(0, B, step=PANEL, unroll=True)
        def _(r):
            rows = pl.ds(pl.multiple_of(r, PANEL), PANEL)
            part = acc[rows, cols] + jnp.dot(
                half[rows, inner], rv[inner, cols], preferred_element_type=jnp.float32
            )
            square = part * part
            for j in range(0, width, 128):
                psq[...] += fold(square[:, j : j + 128])
            pst[rows, cols] = part.astype(jnp.bfloat16)

    def send_back(c):
        for o in (1, 2, 3):
            by_copy(c, o).start()
        yr[c][m] = pst[block_rows(m, c), part_cols(c)]

    right_product(0, W)
    for k in range(HALVES):
        send_back(k)
    right_product(W, W)
    for p in range(1, B // PANEL):
        right_product(p * PANEL, PANEL)
    count = 1.0 / (B * B)
    grad_mean = jnp.sum(gsq[...], axis=(0, 1), keepdims=True) * count
    pre_mean = jnp.sum(psq[...], axis=(0, 1), keepdims=True) * count
    scale = jnp.broadcast_to(jnp.sqrt(grad_mean / (pre_mean + 1e-6)), (8, 128))
    sc_out[...] = scale
    sc_in[m] = scale
    for o in (1, 2, 3):
        sc_copy(o).start()
    for k in range(HALVES, STEPS):
        send_back(k)

    def left_gram(p):
        cols = pl.ds(p * PANEL, PANEL)

        @pl.loop(0, B, step=PANEL, unroll=True)
        def _(r):
            rows = pl.ds(pl.multiple_of(r, PANEL), PANEL)
            nl[rows, cols] += lax.dot_general(
                g[rows, :], g[cols, :], (((1,), (1,)), ((), ())), preferred_element_type=jnp.float32
            )

    def right_gram(p):
        cols = pl.ds(p * PANEL, PANEL)

        @pl.loop(0, B, step=PANEL, unroll=True)
        def _(r):
            rows = pl.ds(pl.multiple_of(r, PANEL), PANEL)
            nr[rows, cols] += jnp.dot(gt[rows, :], g[:, cols], preferred_element_type=jnp.float32)

    loads[2].wait()
    loads[3].wait()

    @pl.loop(0, B, step=PANEL, unroll=True)
    def _(r):
        rows = pl.ds(pl.multiple_of(r, PANEL), PANEL)
        gt[rows, :] = g[:, rows].T

    slots = [slot[z, q, row_block] for q in range(GROUP)]

    def relay_back(c):
        for o in (1, 2, 3):
            by_copy(c, o).wait_recv()
        for o in (2, 1, 3, 0):
            t = z_peers[o]
            q = jnp.int32(0)
            for other in range(1, GROUP):
                q = jnp.where(slots[other] == t, other, q)
            piece = (yr[c][q].astype(jnp.float32) * sc_in[q][0:1, :]).astype(jnp.bfloat16)
            if o:
                zst[c][o - 1] = piece
                bz_copy(c, o).start()
            else:
                upd[z, part_rows(c), part_cols(c)] = piece

    for o in (1, 2, 3):
        sc_copy(o).wait_recv()
    for k in range(STEPS):
        relay_back(k)
        if k % 2 == 0 and k < 8:
            left_gram(k // 2)
        elif k % 2 == 0 and k < 16:
            right_gram(k // 2 - 4)
        for o in (1, 2, 3):
            z_copy(k, o).wait_send()
            y_copy(k, o).wait_send()
            if k:
                by_copy(k - 1, o).wait_send()
    for o in (1, 2, 3):
        sc_copy(o).wait_send()
        by_copy(STEPS - 1, o).wait_send()
    for k in range(STEPS):
        for o in (1, 2, 3):
            bz_copy(k, o).wait()


def write_out(upd, nl, nr, update, new_left, new_right, sem):
    copies = [
        (upd.at[e], update.at[:, pl.ds(e * B, B)]) for e in range(TENSORS)
    ]
    for i in range(4):
        rows = pl.ds(i * ROWS, ROWS)
        copies.append((nl.at[rows], new_left.at[0, rows]))
        copies.append((nr.at[rows], new_right.at[0, rows]))
    copies = [pltpu.make_async_copy(a, b, sem.at[i]) for i, (a, b) in enumerate(copies)]
    for copy in copies:
        copy.start()
    for copy in copies:
        copy.wait()


def per_device(gradient, block_slot, left_factor, right_factor, left_root, right_root):
    vmem, hbm = pl.BlockSpec(memory_space=pltpu.VMEM), pl.BlockSpec(memory_space=pltpu.HBM)
    bf16, f32 = jnp.bfloat16, jnp.float32
    dma = pltpu.SemaphoreType.DMA
    parts = pl.pallas_call(
        kernel,
        out_shape=(
            pltpu.VMEM((TENSORS, ROWS, B), bf16),
            pltpu.VMEM((B, B), f32),
            pltpu.VMEM((B, B), f32),
        ),
        in_specs=[hbm, hbm, hbm, hbm, hbm, hbm],
        out_specs=(vmem, vmem, vmem),
        scratch_shapes=[pltpu.VMEM((4, PART, W), bf16)] * STEPS
        + [pltpu.VMEM((3, PART, W), bf16)] * STEPS
        + [pltpu.VMEM((4, PART, W), bf16)] * STEPS
        + [pltpu.VMEM((3, PART, W), bf16)] * STEPS
        + [pltpu.VMEM((B, B), bf16)] * 6
        + [pltpu.VMEM((8, 128), f32)] * 3
        + [pltpu.VMEM((4, 8, 128), f32)]
        + [pltpu.SMEM((TENSORS, GROUP, block_slot.shape[0]), jnp.int32), dma]
        + [pltpu.VMEM((B, B), f32)]
        + [dma((4,)), dma((STEPS,))]
        + [dma((STEPS, 3))] * 6
        + [dma((4,))] * 2
        + [dma((STEPS, 3))] * 2,
        compiler_params=pltpu.CompilerParams(
            collective_id=0, has_side_effects=True, vmem_limit_bytes=32 * 2**20
        ),
        name="shampoo",
    )(
        *[
            pltpu.with_memory_space_constraint(x, pltpu.HBM)
            for x in (block_slot.transpose(1, 2, 0), gradient, left_factor, right_factor, left_root, right_root)
        ],
    )
    return pl.pallas_call(
        write_out,
        out_shape=(
            pltpu.HBM((ROWS, TENSORS * B), bf16),
            pltpu.HBM((1, B, B), f32),
            pltpu.HBM((1, B, B), f32),
        ),
        in_specs=[vmem] * 3,
        out_specs=[hbm] * 3,
        scratch_shapes=[dma((12,))],
        compiler_params=pltpu.CompilerParams(vmem_limit_bytes=2**20),
        name="write_out",
    )(*[pltpu.with_memory_space_constraint(x, pltpu.VMEM) for x in parts])


def solution(mesh):
    owned = P(("dp", "tensor"), None, None)
    return jax.shard_map(
        per_device,
        mesh=mesh,
        in_specs=(P("dp", "tensor"), P(), owned, owned, owned, owned),
        out_specs=(P("dp", "tensor"), owned, owned),
        check_vma=False,
    )
```
